1024 devices in a mesh: grp: 32 (over z), rep: 32 (over y, x, core).
Axes of the slice: x: 4, y: 4, z: 32, core: 2. Of those that a mesh axis runs over, the one named last changes fastest.
Arguments:
- item_factors: float32 [16384, 256], P('grp')
- light_factors: float32 [16384, 256], P(('grp', 'rep')), may hold values from -3 to 3
- heavy_factors: float32 [1024, 256], P('grp'), may hold values from -3 to 3
- requests: int32 [32768, 16], P(('grp', 'rep')), may hold values from 0 to 511
- counts: int32 [1024, 32], P(('grp', 'rep')), may hold values from 1 to 16, as said below
- slots: int32 [4194304], P(('grp', 'rep')), may hold values from 0 to 511
- confidence: float32 [4194304], P(('grp', 'rep')), may hold values from 1 to 10
- block_user: int32 [32768], P(('grp', 'rep')), may hold values from 0 to 47, as said below
- column_block: int32 [1], replicated, may hold values from 0 to 3
Outputs:
- light_new: float32 [16384, 256], P(('grp', 'rep'))
- heavy_new: float32 [1024, 256], P(('grp', 'rep'))
The draws below stay inside these ranges and needn't reach their ends.
Inputs may be any that keep to these rules, and one draw needn't show every extreme that they name: `counts`: each count lies in 1 to 16; in every group one owner receives 16 live requests from every device of the group. `block_user`: values below 16 name the device's own light users, each of which has a block; 16 + h names heavy user h of the device's group.
All inputs are finite; a program needn't handle non-finite values.
Results may differ from the reference program's by a relative error of at most 0.0003.
Values sent between devices are 32-bit elements; how exact they have to be, the bound alone decides.
A program may use at most 32 MiB of HBM per device.

```python
import math
import jax
import jax.numpy as jnp
from jax import lax

K = 256
BLOCK_COLS = 64
ROWS_BLK = 128
ITEM_DEV = 512
CAP = 16
NBLK = 32
LIGHT_DEV = 16
ITEMS = 16384
HEAVY = 32
USERS = 16384
N_GRP = 32
N_REP = 32


def draw_item_factors(key, part):
    key = jax.random.fold_in(key, 11)
    key_noise, key_row, key_col = jax.random.split(key, 3)
    noise = jax.random.normal(key_noise, (ITEMS, K), jnp.float32)
    rise_factor = 3.0
    row_scale = jnp.exp(jax.random.uniform(key_row, (ITEMS, 1), jnp.float32, math.log(0.4), math.log(4.0)))
    col_scale = jnp.exp(jax.random.uniform(key_col, (1, K), jnp.float32, math.log(0.4), math.log(4.0)))
    owner_count = ITEMS // ITEM_DEV
    position = (jnp.arange(ITEMS, dtype=jnp.int32) // ITEM_DEV).astype(jnp.float32) / max(owner_count - 1, 1)
    shard_scale = jnp.exp(0.5 * math.log(rise_factor) * position)[:, None]
    return noise * row_scale * col_scale * shard_scale / 16.0


def draw_counts(key, part):
    key = jax.random.fold_in(key, 12)
    key_full, key_count = jax.random.split(key)
    senders = N_GRP * N_REP
    full_owner = jax.random.randint(key_full, (N_GRP,), 0, N_GRP, dtype=jnp.int32)
    drawn = jax.random.randint(key_count, (senders, N_GRP), 1, CAP + 1, dtype=jnp.int32)
    sender_group = jnp.arange(senders, dtype=jnp.int32) // N_REP
    marked = jnp.arange(N_GRP, dtype=jnp.int32)[None, :] == jnp.take(full_owner, sender_group)[:, None]
    return jnp.where(marked, CAP, drawn).astype(jnp.int32)


def draw_block_user(key, part):
    key = jax.random.fold_in(key, 13)
    total = N_GRP * N_REP * NBLK
    position = jnp.arange(total, dtype=jnp.int32) % NBLK
    drawn = jax.random.randint(key, (total,), 0, LIGHT_DEV + HEAVY, dtype=jnp.int32)
    return jnp.where(position < LIGHT_DEV, position, drawn).astype(jnp.int32)


def with_ends(result, key, low, top_value):
    dims = result.shape
    place = [jax.random.randint(jax.random.fold_in(key, axis), (), 0, dims[axis]) for axis in range(len(dims))]
    result = result.at[tuple(place)].set(low)
    longest = dims.index(max(dims))
    place[longest] = (place[longest] + 1) % dims[longest]
    return result.at[tuple(place)].set(top_value)


def block_scale(rng, shape, cuts, smallest, high):
    gain, own = 1.0, jax.random.fold_in(rng, 6)
    for dim, blocks in cuts:
        draws = jnp.exp(jax.random.uniform(jax.random.fold_in(own, dim), (blocks,), jnp.float32, smallest / len(cuts), high / len(cuts)))
        gain = gain * jnp.repeat(draws, shape[dim] // blocks).reshape([-1 if axis == dim else 1 for axis in range(len(shape))])
    return gain


def normal_values(key, extent, deviation, reach, pieces=(), kind=jnp.bfloat16):
    values = jax.random.normal(key, extent, jnp.float32) * deviation
    if len(pieces) > 0:
        values = block_scale(key, extent, pieces, -0.22, 0.18) * values
    return jnp.clip(values, min=-reach, max=reach).astype(kind)


def setup_inputs(seed: int = 0) -> dict:
    arg_keys = jax.random.split(jax.random.key(seed), 10)
    item_factors = draw_item_factors(jax.random.fold_in(arg_keys[9], 71), 0)
    light_factors = normal_values(arg_keys[1], (USERS, K), 0.5, 3.0, ((0, 1024),), jnp.float32)
    heavy_factors = normal_values(arg_keys[2], (N_GRP * HEAVY, K), 0.5, 3.0, ((0, 32),), jnp.float32)
    requests = with_ends(jax.random.randint(arg_keys[3], (N_GRP * N_REP * N_GRP, CAP), 0, ITEM_DEV), jax.random.fold_in(arg_keys[3], 1), 0, ITEM_DEV - 1).astype(jnp.int32)
    counts = draw_counts(jax.random.fold_in(arg_keys[9], 71), 0)
    slots = with_ends(jax.random.randint(arg_keys[5], (N_GRP * N_REP * NBLK * ROWS_BLK,), 0, N_GRP * CAP), jax.random.fold_in(arg_keys[5], 1), 0, (N_GRP * CAP) - 1).astype(jnp.int32)
    confidence = jnp.clip(jnp.exp(math.log(10.0) - 2.3025851 * jax.random.uniform(arg_keys[6], (N_GRP * N_REP * NBLK * ROWS_BLK,), jnp.float32) ** block_scale(arg_keys[6], (N_GRP * N_REP * NBLK * ROWS_BLK,), ((0, 1024),), -0.2, 0.2)), 1.0, 10.0)
    block_user = draw_block_user(jax.random.fold_in(arg_keys[9], 71), 0)
    column_block = jax.random.randint(arg_keys[8], (1,), 0, K // BLOCK_COLS).astype(jnp.int32)
    return dict(item_factors=item_factors, light_factors=light_factors, heavy_factors=heavy_factors, requests=requests, counts=counts, slots=slots, confidence=confidence, block_user=block_user, column_block=column_block)


unobserved = 128.0
ridge_weight = 1.0

def refine(factor_rows, normal, right, item_gram, column_start, prior_weight):
    gram_cols = lax.dynamic_slice_in_dim(item_gram, column_start, BLOCK_COLS, 1)
    gram_block = lax.dynamic_slice_in_dim(gram_cols, column_start, BLOCK_COLS, 0)
    old_block = lax.dynamic_slice_in_dim(factor_rows, column_start, BLOCK_COLS, 1)
    gram_user = jnp.dot(factor_rows.astype(jnp.float32), gram_cols.astype(jnp.float32), preferred_element_type=jnp.float32, precision=lax.Precision.HIGHEST)
    system = normal + prior_weight * gram_block + ridge_weight * jnp.eye(BLOCK_COLS, dtype=normal.dtype)
    right_side = right - prior_weight * gram_user - ridge_weight * old_block
    factor = jnp.linalg.cholesky(system)
    middle = lax.linalg.triangular_solve(factor, right_side[..., None], left_side=True, lower=True)
    update = lax.linalg.triangular_solve(factor, middle, left_side=True, lower=True, transpose_a=True)[..., 0]
    return lax.dynamic_update_slice_in_dim(factor_rows, old_block + update, column_start, 1)

def reference(item_factors, light_factors, heavy_factors, requests, counts, slots, confidence, block_user, column_block):
    item_gram = jnp.dot(item_factors.T.astype(jnp.float32), item_factors.astype(jnp.float32), preferred_element_type=jnp.float32, precision=lax.Precision.HIGHEST)
    column_start = column_block[0] * BLOCK_COLS
    prior_weight = unobserved / ITEMS
    user_count = LIGHT_DEV + HEAVY
    rows_dev = NBLK * ROWS_BLK
    offsets = jnp.arange(N_GRP, dtype=jnp.int32) * ITEM_DEV

    def group_update(group_index):
        heavy_rows = lax.dynamic_slice_in_dim(heavy_factors, group_index * HEAVY, HEAVY, 0)

        def device_terms(carry, member):
            device = group_index * N_REP + member
            asked_ids = lax.dynamic_slice_in_dim(requests, device * N_GRP, N_GRP, 0)
            fetched_flat = jnp.take(item_factors, (asked_ids + offsets[:, None]).reshape(-1), axis=0)
            slot_ids = lax.dynamic_slice_in_dim(slots, device * rows_dev, rows_dev, 0)
            item_rows = jnp.take(fetched_flat, slot_ids, axis=0)
            owners = lax.dynamic_slice_in_dim(block_user, device * NBLK, NBLK, 0)
            light_rows = lax.dynamic_slice_in_dim(light_factors, device * LIGHT_DEV, LIGHT_DEV, 0)
            user_rows = jnp.concatenate([light_rows, heavy_rows], 0)
            row_owner = jnp.repeat(owners, ROWS_BLK)
            predicted = jnp.sum(jnp.take(user_rows, row_owner, axis=0) * item_rows, axis=1)
            live_limit = jnp.take(lax.dynamic_slice_in_dim(counts, device, 1, 0)[0], slot_ids // CAP)
            weight = lax.dynamic_slice_in_dim(confidence, device * rows_dev, rows_dev, 0) * (slot_ids % CAP < live_limit).astype(jnp.float32)
            item_block = lax.dynamic_slice_in_dim(item_rows, column_start, BLOCK_COLS, 1).reshape(NBLK, ROWS_BLK, BLOCK_COLS)
            weight_blocks = weight.reshape(NBLK, ROWS_BLK)
            residual = (weight * (1.0 - predicted)).reshape(NBLK, ROWS_BLK)
            block_normal = jnp.einsum('nrk,nrl->nkl', item_block * weight_blocks[..., None], item_block, precision=lax.Precision.HIGHEST)
            block_right = jnp.einsum('nr,nrk->nk', residual, item_block, precision=lax.Precision.HIGHEST)
            user_normal = jax.ops.segment_sum(block_normal, owners, num_segments=user_count)
            user_right = jax.ops.segment_sum(block_right, owners, num_segments=user_count)
            carry = (carry[0] + user_normal[LIGHT_DEV:], carry[1] + user_right[LIGHT_DEV:])
            return (carry, (light_rows, user_normal[:LIGHT_DEV], user_right[:LIGHT_DEV]))
        start_sums = (jnp.zeros((HEAVY, BLOCK_COLS, BLOCK_COLS), jnp.float32), jnp.zeros((HEAVY, BLOCK_COLS), jnp.float32))
        (heavy_normal, heavy_right), (light_rows, light_normal, light_right) = lax.scan(device_terms, start_sums, jnp.arange(N_REP, dtype=jnp.int32))
        all_rows = jnp.concatenate([light_rows.reshape(-1, K), heavy_rows], 0)
        all_normal = jnp.concatenate([light_normal.reshape(-1, BLOCK_COLS, BLOCK_COLS), heavy_normal], 0)
        all_right = jnp.concatenate([light_right.reshape(-1, BLOCK_COLS), heavy_right], 0)
        updated = refine(all_rows, all_normal, all_right, item_gram, column_start, prior_weight)
        return (updated[:N_REP * LIGHT_DEV], updated[N_REP * LIGHT_DEV:])
    light_new, heavy_new = lax.map(group_update, jnp.arange(N_GRP, dtype=jnp.int32))
    return (light_new.reshape(-1, K), heavy_new.reshape(-1, K))
```

```python
import functools

import jax
import jax.numpy as jnp
from jax import lax
from jax.experimental import pallas as pl
from jax.experimental.pallas import tpu as pltpu
from jax.sharding import PartitionSpec as P

COLS = 64
RANK = 256
SLOTS = 512
CAP = 16
LIGHT = 16
HEAVY = 32
TILE = 8
PANELS = COLS // TILE
UNOBSERVED = 128.0
MESH = pl.DeviceIdType.MESH
F32 = jnp.float32
BF16 = jnp.bfloat16
HIGHEST = lax.Precision.HIGHEST
VMEM = pl.BlockSpec(memory_space=pltpu.VMEM)
SMEM = pl.BlockSpec(memory_space=pltpu.SMEM)
LIMIT = 48 * 1024 * 1024

WIDTH = [COLS - TILE * b for b in range(PANELS)]
START = [sum(TILE * w for w in WIDTH[:b]) for b in range(PANELS)]
ENTRIES = sum(TILE * w for w in WIDTH)
LINES = ENTRIES // 128
MESSAGE = 24


def iota(shape, dim):
    return lax.broadcasted_iota(jnp.int32, shape, dim)


def rows_by_rows(a, b, precision=HIGHEST):
    return lax.dot_general(a, b, (((1,), (1,)), ((), ())), precision=precision, preferred_element_type=F32)


def split(x, parts):
    out = []
    for _ in range(parts):
        part = x.astype(BF16)
        out.append(part)
        x = x - part.astype(F32)
    return out


def picker(column_block):
    return (iota((COLS, RANK), 1) == iota((COLS, RANK), 0) + column_block * COLS).astype(F32)


def exact_one_hot_dot(one_hot, x):
    hot = one_hot.astype(BF16)
    return sum(jnp.dot(hot, part, preferred_element_type=F32) for part in split(x, 3))


def fetch_kernel(
    n,
    items_total,
    cb_ref,
    user_ref,
    items_ref,
    req_ref,
    slots_ref,
    conf_ref,
    h_ref,
    gram_ref,
    c_ref,
    ring,
    owned,
    answer,
    ask_out,
    ask_in,
    part_out,
    part_in,
    sum_out,
    sum_in,
    weight_sum,
    right_s,
    right_r,
    left_s,
    left_r,
    own_s,
    own_r,
    ask_s,
    ask_r,
    ans_s,
    ans_r,
    part_s,
    part_r,
    sum_s,
    sum_r,
):
    g, r = lax.axis_index("grp"), lax.axis_index("rep")
    right, left = lax.rem(g + 1, n), lax.rem(g + n - 1, n)
    share = ring.shape[1]

    def put(src, dst, send, recv, target):
        return pltpu.make_async_remote_copy(
            src_ref=src, dst_ref=dst, send_sem=send, recv_sem=recv, device_id=target, device_id_type=MESH
        )

    def peers(body):
        def one(k, carry):
            body(lax.rem(r + k, n))
            return carry

        lax.fori_loop(1, n, one, 0)

    barrier = pltpu.get_barrier_semaphore()
    peers(lambda p: pl.semaphore_signal(barrier, inc=1, device_id=(g, p), device_id_type=MESH))
    pl.semaphore_signal(barrier, inc=1, device_id=(left, r), device_id_type=MESH)
    pl.semaphore_signal(barrier, inc=1, device_id=(right, r), device_id_type=MESH)
    ring[g] = items_ref[pl.ds(pl.multiple_of(r * share, share), share), :]
    spread = (
        (iota((CAP, 128), 1) % CAP == iota((CAP, 128), 0)) & (iota((CAP, 128), 1) // CAP == lax.rem(r, TILE))
    ).astype(F32)
    asked = jnp.dot(req_ref[...].astype(F32), spread, precision=HIGHEST, preferred_element_type=F32)
    for p in range(n):
        ask_out[p] = asked[p : p + 1, :]
    weight_sum[...] = jnp.zeros_like(weight_sum)
    pl.semaphore_wait(barrier, n + 1)

    def go_right(t):
        p = lax.rem(g + n - t, n)
        return put(ring.at[p], ring.at[p], right_s.at[t], right_r.at[t], (right, r))

    def go_left(t):
        p = lax.rem(g + t, n)
        return put(ring.at[p], ring.at[p], left_s.at[t], left_r.at[t], (left, r))

    def came_right(t):
        p = lax.rem(g + n - t - 1, n)
        put(ring.at[p], ring.at[p], right_s.at[t], right_r.at[t], (right, r)).wait_recv()
        return p

    def came_left(t):
        p = lax.rem(g + t + 1, n)
        put(ring.at[p], ring.at[p], left_s.at[t], left_r.at[t], (left, r)).wait_recv()
        return p

    def to_owner(p):
        return put(ring.at[p], owned.at[r], own_s.at[p], own_r.at[r], (g, p))

    def hand_over(p):
        @pl.when(p != r)
        def _():
            to_owner(p).start()

        @pl.when(p == r)
        def _():
            owned[r] = ring[p]

    def ask(p):
        return put(ask_out.at[p], ask_in.at[r], ask_s.at[p], ask_r.at[r], (g, p))

    def asked_by(p):
        return put(ask_out.at[p], ask_in.at[p], ask_s.at[p], ask_r.at[p], (g, p))

    def weigh(step):
        hot, parts = [], [[], [], []]
        for half in range(2):
            row = 2 * step + half
            slot = slots_ref[pl.ds(row, 1), :]
            hot.append((iota((SLOTS, 128), 0) == slot).astype(F32).astype(BF16))
            user = (iota((LIGHT + HEAVY, 128), 0) == user_ref[row]).astype(F32)
            for k, part in enumerate(split(conf_ref[pl.ds(row, 1), :], 3)):
                parts[k].append(user * part.astype(F32))
        lhs = jnp.concatenate([jnp.concatenate(p, 1) for p in parts], 0).astype(BF16)
        weight_sum[...] += rows_by_rows(lhs, jnp.concatenate(hot, 1), None)

    half = n // 2
    go_right(0).start()
    go_left(0).start()
    hand_over(g)
    peers(lambda p: ask(p).start())
    ask_in[r] = ask_out[r]

    def ring_step(t, carry):
        p = came_right(t - 1)
        go_right(t).start()
        q = came_left(t - 1)

        @pl.when(t < half - 1)
        def _():
            go_left(t).start()

        hand_over(p)
        hand_over(q)
        weigh(t - 1)
        return carry

    lax.fori_loop(1, half, ring_step, 0)
    hand_over(came_right(half - 1))
    weigh(half - 1)

    peers(lambda p: asked_by(p).wait_recv())
    lines = [jnp.sum(ask_in[TILE * q : TILE * q + TILE], axis=0) for q in range(n // TILE)]
    lines = jnp.concatenate(lines + [jnp.zeros((TILE - len(lines), 128), F32)], 0)
    eye = (iota((128, 128), 0) == iota((128, 128), 1)).astype(F32)
    wanted = rows_by_rows(eye, lines)
    hots = [(wanted[:, q : q + 1] == iota((128, SLOTS), 1).astype(F32)).astype(F32) for q in range(n // TILE)]

    def handed_by(p):
        return put(ring.at[p], owned.at[p], own_s.at[p], own_r.at[p], (g, p))

    def reply(p):
        return put(answer.at[p], h_ref.at[r], ans_s.at[p], ans_r.at[r], (g, p))

    def replied_by(p):
        return put(answer.at[p], h_ref.at[p], ans_s.at[p], ans_r.at[p], (g, p))

    peers(lambda p: handed_by(p).wait_recv())
    rows = owned[...].reshape(n * share, RANK)
    for q, hot in enumerate(hots):
        answer[TILE * q : TILE * q + TILE] = exact_one_hot_dot(hot, rows).reshape(TILE, CAP, RANK)
    peers(lambda p: reply(p).start())
    h_ref[r] = answer[r]

    mine = ring[...].reshape(n * share, RANK)
    pick = picker(cb_ref[0])
    mine_cols = rows_by_rows(pick, mine)
    part = jnp.dot(mine_cols, mine, precision=HIGHEST, preferred_element_type=F32)
    for k in range(n):
        a, b, c = k // 4, (k // 2) % 2, k % 2
        part_out[k] = part[8 * a + 4 * c : 8 * a + 4 * c + 4, 128 * b : 128 * b + 128]

    def give(p):
        return put(part_out.at[p], part_in.at[r], part_s.at[p], part_r.at[r], (g, p))

    def given_by(p):
        return put(part_out.at[p], part_in.at[p], part_s.at[p], part_r.at[p], (g, p))

    def share_sum(p):
        return put(sum_out.at[0], sum_in.at[r], sum_s.at[p], sum_r.at[r], (g, p))

    def sum_of(p):
        return put(sum_out.at[0], sum_in.at[p], sum_s.at[p], sum_r.at[p], (g, p))

    peers(lambda p: give(p).start())
    part_in[r] = part_out[r]
    peers(lambda p: given_by(p).wait_recv())
    sum_out[0] = jnp.sum(part_in[...], axis=0)
    peers(lambda p: share_sum(p).start())
    sum_in[r] = sum_out[0]
    users = LIGHT + HEAVY
    c_ref[...] = weight_sum[:users] + weight_sum[users : 2 * users] + weight_sum[2 * users :]
    peers(lambda p: sum_of(p).wait_recv())
    for k in range(n):
        a, b, c = k // 4, (k // 2) % 2, k % 2
        gram_ref[8 * a + 4 * c : 8 * a + 4 * c + 4, 128 * b : 128 * b + 128] = sum_in[k]
    peers(lambda p: replied_by(p).wait_recv())

    def sent_right(t, carry):
        go_right(t).wait_send()
        return carry

    def sent_left(t, carry):
        go_left(t).wait_send()
        return carry

    lax.fori_loop(0, half, sent_right, 0)
    lax.fori_loop(0, half - 1, sent_left, 0)
    for sent in (to_owner, ask, reply, give, share_sum):
        peers(lambda p, sent=sent: sent(p).wait_send())


def fetch(n, items, requests, slots, confidence, block_user, column_block):
    share = items.shape[0] // n
    dma = [pltpu.SemaphoreType.DMA((n,)) for _ in range(14)]
    users = LIGHT + HEAVY
    return pl.pallas_call(
        functools.partial(fetch_kernel, n, items.shape[0] * n),
        out_shape=(
            jax.ShapeDtypeStruct((n, CAP, RANK), F32),
            jax.ShapeDtypeStruct((COLS, RANK), F32),
            jax.ShapeDtypeStruct((users, SLOTS), F32),
        ),
        in_specs=[SMEM, SMEM, VMEM, VMEM, VMEM, VMEM],
        out_specs=(VMEM, VMEM, VMEM),
        scratch_shapes=[
            pltpu.VMEM((n, share, RANK), F32),
            pltpu.VMEM((n, share, RANK), F32),
            pltpu.VMEM((n, CAP, RANK), F32),
            pltpu.VMEM((n, 1, 128), F32),
            pltpu.VMEM((n, 1, 128), F32),
            pltpu.VMEM((n, 4, 128), F32),
            pltpu.VMEM((n, 4, 128), F32),
            pltpu.VMEM((1, 4, 128), F32),
            pltpu.VMEM((n, 4, 128), F32),
            pltpu.VMEM((3 * users, SLOTS), F32),
            *dma,
        ],
        compiler_params=pltpu.CompilerParams(collective_id=0, has_side_effects=True, vmem_limit_bytes=LIMIT),
        name="fetch",
    )(column_block, block_user, items, requests, slots, confidence)


def normal_kernel(cb_ref, h_ref, c_ref, counts_ref, light_ref, heavy_ref, flat_ref, right_ref, msg_ref):
    users = LIGHT + HEAVY
    rows = h_ref[...].reshape(SLOTS, RANK)
    owners = counts_ref.shape[1]
    by_slot = (iota((owners, SLOTS), 1) // CAP == iota((owners, SLOTS), 0)).astype(BF16)
    limit = jnp.dot(
        jnp.broadcast_to(counts_ref[...], (TILE, owners)).astype(F32).astype(BF16),
        by_slot,
        preferred_element_type=F32,
    )[:1]
    live = (iota((1, SLOTS), 1) % CAP).astype(F32) < limit
    weight = jnp.where(live, c_ref[...], 0.0)
    factors = jnp.concatenate([light_ref[...], heavy_ref[...]], 0)
    residual = weight * (1.0 - rows_by_rows(factors, rows))
    cols = rows_by_rows(picker(cb_ref[0]), rows)
    none = jnp.zeros((64 - users, SLOTS), F32)
    right = rows_by_rows(cols, jnp.concatenate([residual, jnp.zeros((128 - users, SLOTS), F32)], 0))
    right_ref[...] = right
    high, low = [part.astype(F32) for part in split(weight, 2)]
    both = jnp.concatenate([high, none, low, none], 0).astype(BF16)
    once = jnp.concatenate([high, none, jnp.zeros((64, SLOTS), F32)], 0).astype(BF16)
    for b in range(PANELS):
        width = WIDTH[b]
        tail = cols[TILE * b :]
        product = jnp.concatenate([tail * cols[TILE * b + i : TILE * b + i + 1] for i in range(TILE)], 0)
        p_high, p_low = split(product, 2)
        first = rows_by_rows(p_high, both, None)
        second = rows_by_rows(p_low, once, None)
        flat_ref[START[b] : START[b] + TILE * width, :] = first + pltpu.roll(first, 64, 1) + second
    for q in range(LINES):
        turned = flat_ref[128 * q : 128 * q + 128, :].T
        msg_ref[:, q, :] = turned[LIGHT:users]
    turned = jnp.concatenate([right, jnp.zeros((64, 128), F32)], 0).T
    msg_ref[:, LINES, :] = turned[LIGHT:users]
    for q in range(LINES + 1, MESSAGE):
        msg_ref[:, q, :] = jnp.zeros((HEAVY, 128), F32)


def normals(h, c, counts, light, heavy, column_block):
    return pl.pallas_call(
        normal_kernel,
        out_shape=(
            jax.ShapeDtypeStruct((ENTRIES, 128), F32),
            jax.ShapeDtypeStruct((COLS, 128), F32),
            jax.ShapeDtypeStruct((HEAVY, MESSAGE, 128), F32),
        ),
        in_specs=[SMEM, VMEM, VMEM, VMEM, VMEM, VMEM],
        out_specs=(VMEM, VMEM, VMEM),
        compiler_params=pltpu.CompilerParams(vmem_limit_bytes=LIMIT),
        name="normals",
    )(column_block, h, c, counts, light, heavy)


def reduce_kernel(n, msg_ref, out_ref, landed, send, recv):
    g, r = lax.axis_index("grp"), lax.axis_index("rep")

    def peers(body):
        def one(k, carry):
            body(lax.rem(r + k, n))
            return carry

        lax.fori_loop(1, n, one, 0)

    barrier = pltpu.get_barrier_semaphore()
    peers(lambda p: pl.semaphore_signal(barrier, inc=1, device_id=(g, p), device_id_type=MESH))
    pl.semaphore_wait(barrier, n - 1)

    def put(p, slot):
        return pltpu.make_async_remote_copy(
            src_ref=msg_ref.at[p],
            dst_ref=landed.at[slot],
            send_sem=send.at[p],
            recv_sem=recv.at[slot],
            device_id=(g, p),
            device_id_type=MESH,
        )

    peers(lambda p: put(p, r).start())
    landed[r] = msg_ref[r]
    peers(lambda p: put(p, p).wait_recv())
    out_ref[...] = jnp.sum(landed[...], axis=0)
    peers(lambda p: put(p, r).wait_send())


def reduce_heavy(n, message):
    return pl.pallas_call(
        functools.partial(reduce_kernel, n),
        out_shape=jax.ShapeDtypeStruct((MESSAGE, 128), F32),
        in_specs=[VMEM],
        out_specs=VMEM,
        scratch_shapes=[
            pltpu.VMEM((n, MESSAGE, 128), F32),
            pltpu.SemaphoreType.DMA((n,)),
            pltpu.SemaphoreType.DMA((n,)),
        ],
        compiler_params=pltpu.CompilerParams(collective_id=1, has_side_effects=True, vmem_limit_bytes=LIMIT),
        name="reduce_heavy",
    )(message)


def solve_kernel(
    prior,
    cb_ref,
    flat_ref,
    right_ref,
    heavy_sum_ref,
    gram_ref,
    light_ref,
    heavy_ref,
    light_out,
    heavy_out,
    a_ref,
    l_ref,
    inv_ref,
    x_ref,
):
    r = lax.axis_index("rep")
    pick = picker(cb_ref[0])
    own = heavy_ref[pl.ds(r, 1), :]
    factors = jnp.concatenate([light_ref[...], own, jnp.zeros((128 - LIGHT - 1, RANK), F32)], 0)
    gram = prior * gram_ref[...]
    block = rows_by_rows(gram, pick) + (iota((COLS, COLS), 0) == iota((COLS, COLS), 1)).astype(F32)
    pulled = rows_by_rows(gram + pick, factors)
    turned = jnp.concatenate([heavy_sum_ref[...], jnp.zeros((128 - MESSAGE, 128), F32)], 0).T
    lane = iota((1, 128), 1)
    is_light, is_heavy = lane < LIGHT, lane == LIGHT
    right = jnp.where(is_light, right_ref[...], jnp.where(is_heavy, turned[:COLS, LINES : LINES + 1], 0.0)) - pulled
    for q in range(LINES):
        part = flat_ref[128 * q : 128 * q + 128, :]
        flat_ref[128 * q : 128 * q + 128, :] = jnp.where(
            is_light, part, jnp.where(is_heavy, turned[:, q : q + 1], 0.0)
        )
    for i in range(COLS):
        b = i // TILE
        at = START[b] + (i - TILE * b) * WIDTH[b]
        a_ref[i, TILE * b : COLS, :] = flat_ref[at : at + WIDTH[b], :] + block[TILE * b :, i : i + 1]
        a_ref[i, COLS : COLS + TILE, :] = jnp.broadcast_to(right[i : i + 1, :], (TILE, 128))

    tiles = PANELS + 1
    for b in range(PANELS):
        base = TILE * b
        acc = {
            (k, t): a_ref[base + k, TILE * t : TILE * t + TILE, :] for k in range(TILE) for t in range(b, tiles)
        }
        for k in range(TILE):
            own_tile = acc[k, b]
            inv = 1.0 / jnp.broadcast_to(own_tile[k : k + 1], (TILE, 128))
            inv_ref[base + k] = inv
            for t in range(b, tiles):
                if t > b:
                    a_ref[base + k, TILE * t : TILE * t + TILE, :] = acc[k, t]
                    if t < PANELS:
                        l_ref[base + k, TILE * t : TILE * t + TILE, :] = acc[k, t] * inv
            a_ref[base + k, base : base + TILE, :] = own_tile
            for k2 in range(k + 1, TILE):
                factor = jnp.broadcast_to(own_tile[k2 : k2 + 1], (TILE, 128)) * inv
                for t in range(b, tiles):
                    acc[k2, t] = acc[k2, t] - factor * acc[k, t]
        for s in range(b + 1, PANELS):
            for k2 in range(TILE):
                row = TILE * s + k2
                factors_ = [
                    jnp.broadcast_to(l_ref[base + k, row : row + 1, :], (TILE, 128)) for k in range(TILE)
                ]
                for t in range(s, tiles):
                    total = a_ref[row, TILE * t : TILE * t + TILE, :]
                    for k in range(TILE):
                        total = total - factors_[k] * a_ref[base + k, TILE * t : TILE * t + TILE, :]
                    a_ref[row, TILE * t : TILE * t + TILE, :] = total

    x = [None] * PANELS
    place = iota((TILE, 128), 0)
    for b in reversed(range(PANELS)):
        base = TILE * b
        left = []
        for k in range(TILE):
            value = a_ref[base + k, COLS : COLS + TILE, :]
            if b + 1 < PANELS:
                total = sum(
                    a_ref[base + k, TILE * t : TILE * t + TILE, :] * x[t] for t in range(b + 1, PANELS)
                )
                value = value - jnp.sum(total, axis=0, keepdims=True)
            left.append(value)
        found = jnp.zeros((TILE, 128), F32)
        for k in reversed(range(TILE)):
            value = left[k] * inv_ref[base + k]
            found = jnp.where(place == k, value, found)
            for k2 in range(k):
                left[k2] = left[k2] - jnp.broadcast_to(a_ref[base + k2, base + k : base + k + 1, :], (TILE, 128)) * value
        x[b] = found
        x_ref[base : base + TILE, :] = found
    x_ref[COLS:, :] = jnp.zeros((128 - COLS, 128), F32)
    delta = x_ref[...].T[:, :COLS]
    delta = jnp.concatenate([delta, delta, delta, delta], 1)
    inside = iota((1, RANK), 1) // COLS == cb_ref[0]
    light_out[...] = light_ref[...] + jnp.where(inside, delta[:LIGHT], 0.0)
    heavy_out[...] = own + jnp.where(inside, delta[LIGHT : LIGHT + 1], 0.0)


def solve(prior, flat, right, heavy_sum, gram, light, heavy, column_block):
    return pl.pallas_call(
        functools.partial(solve_kernel, prior),
        out_shape=(jax.ShapeDtypeStruct((LIGHT, RANK), F32), jax.ShapeDtypeStruct((1, RANK), F32)),
        in_specs=[SMEM, VMEM, VMEM, VMEM, VMEM, VMEM, VMEM],
        out_specs=(VMEM, VMEM),
        scratch_shapes=[
            pltpu.VMEM((COLS, COLS + TILE, 128), F32),
            pltpu.VMEM((COLS, COLS, 128), F32),
            pltpu.VMEM((COLS, TILE, 128), F32),
            pltpu.VMEM((128, 128), F32),
        ],
        compiler_params=pltpu.CompilerParams(vmem_limit_bytes=LIMIT),
        name="solve",
    )(column_block, flat, right, heavy_sum, gram, light, heavy)


def local(items, light, heavy, requests, counts, slots, confidence, block_user, column_block):
    n = lax.axis_size("grp")
    blocks = block_user.shape[0]
    h, gram, c = fetch(
        n,
        items,
        requests,
        slots.reshape(blocks, -1),
        confidence.reshape(blocks, -1),
        block_user,
        column_block,
    )
    flat, right, message = normals(h, c, counts, light, heavy, column_block)
    heavy_sum = reduce_heavy(lax.axis_size("rep"), message)
    prior = UNOBSERVED / (items.shape[0] * n)
    return solve(prior, flat, right, heavy_sum, gram, light, heavy, column_block)


def solution(mesh):
    both = ("grp", "rep")
    return jax.shard_map(
        local,
        mesh=mesh,
        in_specs=(
            P("grp", None),
            P(both, None),
            P("grp", None),
            P(both, None),
            P(both, None),
            P(both),
            P(both),
            P(both),
            P(),
        ),
        out_specs=(P(both, None), P(both, None)),
        check_vma=False,
    )
```

```python
import functools

import jax
import jax.numpy as jnp
from jax import lax
from jax.experimental import pallas as pl
from jax.experimental.pallas import tpu as pltpu
from jax.sharding import PartitionSpec as P

COLS = 64
RANK = 256
SLOTS = 512
CAP = 16
LIGHT = 16
HEAVY = 32
TILE = 8
PANELS = COLS // TILE
UNOBSERVED = 128.0
MESH = pl.DeviceIdType.MESH
F32 = jnp.float32
BF16 = jnp.bfloat16
HIGHEST = lax.Precision.HIGHEST
VMEM = pl.BlockSpec(memory_space=pltpu.VMEM)
SMEM = pl.BlockSpec(memory_space=pltpu.SMEM)
HBM = pl.BlockSpec(memory_space=pltpu.HBM)
LIMIT = 56 * 1024 * 1024

WIDTH = [COLS - TILE * b for b in range(PANELS)]
START = [sum(TILE * w for w in WIDTH[:b]) for b in range(PANELS)]
ENTRIES = sum(TILE * w for w in WIDTH)
LINES = ENTRIES // 128
MESSAGE = 24

SPINE = [0, 5, 10, 14, -5, -10, -14]
FORWARD = [(1, 0), (4, 0), (2, 1), (5, 4), (3, 2), (6, 5)]
REACH = [0, 5, 10, 14]
LEAVES = [(0, 1, -1, 2, -2)] * 3 + [(2, 1, 0, -1)] + [(0, 1, -1, 2, -2)] * 2 + [(-1, 0, 1)]


def iota(shape, dim):
    return lax.broadcasted_iota(jnp.int32, shape, dim)


def rows_by_rows(a, b, precision=HIGHEST):
    return lax.dot_general(a, b, (((1,), (1,)), ((), ())), precision=precision, preferred_element_type=F32)


def split(x, parts):
    out = []
    for _ in range(parts):
        part = x.astype(BF16)
        out.append(part)
        x = x - part.astype(F32)
    return out


def picker(column_block):
    return (iota((COLS, RANK), 1) == iota((COLS, RANK), 0) + column_block * COLS).astype(F32)


def gather_kernel(
    n,
    cb_ref,
    items_ref,
    req_ref,
    slots_ref,
    conf_ref,
    user_ref,
    counts_ref,
    light_ref,
    heavy_ref,
    flat_out,
    right_ref,
    reduced_ref,
    gram_ref,
    flat_ref,
    heavy_flat,
    load_out,
    load_in,
    sum_out,
    sum_in,
    spine,
    owned,
    answer,
    rows_ref,
    ask_out,
    ask_in,
    part_out,
    part_in,
    msg,
    landed,
    hot_ref,
    by_block,
    req_buf,
    slots_buf,
    conf_buf,
    user_buf,
    counts_buf,
    factors,
    load_sem,
    spine_s,
    spine_r,
    leaf_s,
    own_r,
    ask_s,
    ask_r,
    ans_s,
    ans_r,
    part_s,
    part_r,
    msg_s,
    msg_r,
    load_s,
    load_r,
    sum_s,
    sum_r,
):
    g, r = lax.axis_index("grp"), lax.axis_index("rep")
    share = owned.shape[1]
    users = LIGHT + HEAVY

    def plane(k):
        return lax.rem(g + (k + n), n)

    def put(src, dst, send, recv, target):
        return pltpu.make_async_remote_copy(
            src_ref=src, dst_ref=dst, send_sem=send, recv_sem=recv, device_id=target, device_id_type=MESH
        )

    def peers(body):
        def one(k, carry):
            body(lax.rem(r + k, n))
            return carry

        lax.fori_loop(1, n, one, 0)

    off = lax.rem(g + n - r, n)
    behind = off // (n // 2 + 1)
    size = off + behind * (n - 2 * off)
    level = (size + 2) // 5
    step = 5 * level - level // 3
    source = lax.rem(r + step * (1 - 2 * behind) + n, n)

    barrier = pltpu.get_barrier_semaphore()

    @pl.when(source != g)
    def _():
        def greet(k, carry):
            pl.semaphore_signal(barrier, inc=1, device_id=(source, k), device_id_type=MESH)
            return carry

        lax.fori_loop(0, n, greet, 0)

    for hop in (5, -5, 4, -4):
        pl.semaphore_signal(barrier, inc=1, device_id=(plane(hop), r), device_id_type=MESH)
    peers(lambda p: pl.semaphore_signal(barrier, inc=1, device_id=(g, p), device_id_type=MESH))
    loads = [
        (items_ref.at[pl.ds(pl.multiple_of(r * share, share), share)], spine.at[0]),
        (req_ref, req_buf),
        (slots_ref, slots_buf),
        (conf_ref, conf_buf),
        (user_ref, user_buf),
        (counts_ref, counts_buf),
        (light_ref, factors.at[pl.ds(0, LIGHT)]),
        (heavy_ref, factors.at[pl.ds(LIGHT, HEAVY)]),
    ]
    loads = [pltpu.make_async_copy(src, dst, load_sem.at[k]) for k, (src, dst) in enumerate(loads)]
    for load in loads:
        load.start()

    leaves = [(k, e) for k in range(len(SPINE)) for e in LEAVES[k]]
    loads[1].wait()
    spread = (
        (iota((CAP, 128), 1) % CAP == iota((CAP, 128), 0)) & (iota((CAP, 128), 1) // CAP == lax.rem(r, TILE))
    ).astype(F32)
    asked = lax.dot_general(
        req_buf[...].astype(F32), spread, (((0,), (0,)), ((), ())), precision=HIGHEST, preferred_element_type=F32
    )
    for p in range(n):
        ask_out[p] = asked[p : p + 1, :]
    loads[0].wait()
    pl.semaphore_wait(barrier, n - 1 + 4 + sum(e != 0 for _, e in leaves))

    def ahead(k, from_k):
        hop = SPINE[k] - SPINE[from_k]
        return put(spine.at[from_k], spine.at[k], spine_s.at[k], spine_r.at[k], (plane(hop), r))

    def leaf(index):
        k, e = leaves[index]
        owner = plane(-SPINE[k])
        return owner, put(spine.at[k], owned.at[r], leaf_s.at[index], own_r.at[r], (plane(e), owner))

    def pass_on(k):
        for later, earlier in FORWARD:
            if earlier == k:
                ahead(later, k).start()
        for index, (at, e) in enumerate(leaves):
            if at != k:
                continue
            owner, copy = leaf(index)
            if e != 0:
                copy.start()
                continue

            @pl.when(owner != r)
            def _(copy=copy):
                copy.start()

            @pl.when(owner == r)
            def _():
                owned[r] = spine[k]

    def ask(p):
        return put(ask_out.at[p], ask_in.at[r], ask_s.at[p], ask_r.at[r], (g, p))

    def asked_by(p):
        return put(ask_out.at[p], ask_in.at[p], ask_s.at[p], ask_r.at[p], (g, p))

    pass_on(0)
    peers(lambda p: ask(p).start())
    ask_in[r] = ask_out[r]

    def weigh(step, carry):
        for k in range(4):
            row = 4 * step + k
            slot = slots_buf[pl.ds(row, 1), :]
            parts = [part.astype(F32) for part in split(conf_buf[pl.ds(row, 1), :], 3)]
            place = iota((16, 128), 0)
            parts = jnp.where(
                place < 4, parts[0], jnp.where(place < 8, parts[1], jnp.where(place < 12, parts[2], 0.0))
            )
            lhs = jnp.where((place & 3) == (slot >> 7), parts, 0.0).astype(BF16)
            hot = (iota((128, 128), 0) == (slot & 127)).astype(F32).astype(BF16)
            got = rows_by_rows(lhs, hot, None)
            got = got[0:4] + got[4:8] + got[8:12]
            by_block[pl.ds(row, 1), :] = jnp.concatenate([got[a : a + 1] for a in range(4)], 1)
        return carry

    for load in loads[2:]:
        load.wait()
    lax.fori_loop(0, by_block.shape[0] // 4, weigh, 0)

    peers(lambda p: asked_by(p).wait_recv())
    lines = [jnp.sum(ask_in[TILE * q : TILE * q + TILE], axis=0) for q in range(n // TILE)]
    lines = jnp.concatenate(lines + [jnp.zeros((TILE - len(lines), 128), F32)], 0)
    eye = (iota((128, 128), 0) == iota((128, 128), 1)).astype(F32)
    wanted = rows_by_rows(eye, lines)
    for q in range(n // TILE):
        hot_ref[128 * q : 128 * q + 128, :] = (
            (wanted[:, q : q + 1] == iota((128, SLOTS), 1).astype(F32)).astype(F32).astype(BF16)
        )

    def reply(p):
        return put(answer.at[p], rows_ref.at[r], ans_s.at[p], ans_r.at[r], (g, p))

    def replied_by(p):
        return put(answer.at[p], rows_ref.at[p], ans_s.at[p], ans_r.at[p], (g, p))

    pick = picker(cb_ref[0])

    def give(p):
        return put(part_out.at[p], part_in.at[r], part_s.at[p], part_r.at[r], (g, p))

    def given_by(p):
        return put(part_out.at[p], part_in.at[p], part_s.at[p], part_r.at[p], (g, p))

    def stand_in():
        def arrived(k, carry):
            @pl.when(n * source + k != n * g + r)
            def _():
                put(spine.at[0], owned.at[k], leaf_s.at[0], own_r.at[k], (source, k)).wait_recv()

            return carry

        lax.fori_loop(0, n, arrived, 0)
        parts = split(owned[...].reshape(n * share, RANK), 2)
        half = n // 2

        def block(q, carry):
            at = lax.rem(r // half + 1 + q, 2)
            hot = hot_ref[pl.ds(pl.multiple_of(CAP * half * at, CAP * half), CAP * half), :]
            got = sum(jnp.dot(hot, part, preferred_element_type=F32) for part in parts)
            answer[pl.ds(pl.multiple_of(half * at, half), half)] = got.reshape(half, CAP, RANK)

            def one(k, inner):
                p = half * at + lax.rem(r + k, half)

                @pl.when(p != r)
                def _():
                    reply(p).start()

                @pl.when(p == r)
                def _():
                    rows_ref[r] = answer[r]

                return inner

            return lax.fori_loop(0, half, one, carry)

        lax.fori_loop(0, 2, block, 0)

    def burden(p):
        return put(load_out.at[p], load_in.at[r], load_s.at[p], load_r.at[r], (g, p))

    def burden_of(p):
        return put(load_out.at[p], load_in.at[p], load_s.at[p], load_r.at[p], (g, p))

    for at in range(4):
        if at == 1:
            owners = counts_buf.shape[1]
            by_slot = (iota((owners, SLOTS), 1) // CAP == iota((owners, SLOTS), 0)).astype(F32).astype(BF16)
            limit = jnp.dot(
                jnp.broadcast_to(counts_buf[...], (TILE, owners)).astype(F32).astype(BF16),
                by_slot,
                preferred_element_type=F32,
            )[:1]
            live = (iota((1, SLOTS), 1) % CAP).astype(F32) < limit
            of_user = (iota((users, by_block.shape[0]), 0) == user_buf[...]).astype(F32)
            weight = jnp.dot(of_user, by_block[...], precision=HIGHEST, preferred_element_type=F32)
            weight = jnp.where(live, weight, 0.0)
            light_weight = weight[:LIGHT]
            turned = jnp.concatenate([weight[LIGHT:], jnp.zeros((128 - HEAVY, SLOTS), F32)], 0).T
            load_out[...] = turned.reshape(n, CAP, 128)
            peers(lambda p: burden(p).start())
            load_in[r] = load_out[r]
        if at < 3:
            for later, earlier in FORWARD:
                if abs(SPINE[later]) == REACH[at + 1]:
                    hop = SPINE[later] - SPINE[earlier]
                    put(
                        spine.at[earlier], spine.at[later], spine_s.at[later], spine_r.at[later], (plane(-hop), r)
                    ).wait_recv()
                    pass_on(later)
        if at == 3:
            peers(lambda p: burden_of(p).wait_recv())
            heavy_weight = load_in[...].reshape(n * CAP, 128).T[:HEAVY]
            parts = jnp.concatenate([part.astype(F32) for part in split(heavy_weight, 3)], 0).astype(BF16)
            heavy_weight = jnp.dot(parts, hot_ref[...], preferred_element_type=F32)
            heavy_weight = (
                heavy_weight[:HEAVY] + heavy_weight[HEAVY : 2 * HEAVY] + heavy_weight[2 * HEAVY :]
            )
        pl.when(level == at)(stand_in)

    def sum_of(p):
        return put(sum_out.at[0], sum_in.at[p], sum_s.at[p], sum_r.at[p], (g, p))

    def share_sum(p):
        return put(sum_out.at[0], sum_in.at[r], sum_s.at[p], sum_r.at[r], (g, p))

    def send(p):
        return put(msg.at[p], landed.at[r], msg_s.at[p], msg_r.at[r], (g, p))

    def sent_by(p):
        return put(msg.at[p], landed.at[p], msg_s.at[p], msg_r.at[p], (g, p))

    def normals(into, cols, weight, residual):
        count = weight.shape[0]
        none = jnp.zeros((64 - count, SLOTS), F32)
        high, low = [part.astype(F32) for part in split(weight, 2)]
        both = jnp.concatenate([high, none, low, none], 0).astype(BF16)
        once = jnp.concatenate([high, none, jnp.zeros((64, SLOTS), F32)], 0).astype(BF16)
        for b in range(PANELS):
            width = WIDTH[b]
            tail = cols[TILE * b :]
            product = jnp.concatenate([tail * cols[TILE * b + i : TILE * b + i + 1] for i in range(TILE)], 0)
            p_high, p_low = split(product, 2)
            first = rows_by_rows(p_high, both, None)
            second = rows_by_rows(p_low, once, None)
            into[START[b] : START[b] + TILE * width, :] = first + pltpu.roll(first, 64, 1) + second
        return rows_by_rows(cols, jnp.concatenate([residual, jnp.zeros((128 - count, SLOTS), F32)], 0))

    mine = owned[...].reshape(n * share, RANK)
    cols = rows_by_rows(pick, mine)
    part = jnp.dot(cols, mine, precision=HIGHEST, preferred_element_type=F32)
    for k in range(n):
        a, b, c = k // 4, (k // 2) % 2, k % 2
        part_out[k] = part[8 * a + 4 * c : 8 * a + 4 * c + 4, 128 * b : 128 * b + 128]
    peers(lambda p: give(p).start())
    part_in[r] = part_out[r]

    residual = heavy_weight * (1.0 - rows_by_rows(factors[LIGHT:users, :], mine))
    right = normals(heavy_flat, cols, heavy_weight, residual)
    for q in range(LINES):
        msg[:, q, :] = heavy_flat[128 * q : 128 * q + 128, :].T[:HEAVY]
    msg[:, LINES, :] = jnp.concatenate([right, jnp.zeros((64, 128), F32)], 0).T[:HEAVY]
    for q in range(LINES + 1, MESSAGE):
        msg[:, q, :] = jnp.zeros((HEAVY, 128), F32)
    peers(lambda p: send(p).start())
    landed[r] = msg[r]

    peers(lambda p: given_by(p).wait_recv())
    sum_out[0] = jnp.sum(part_in[...], axis=0)
    peers(lambda p: share_sum(p).start())
    sum_in[r] = sum_out[0]

    peers(lambda p: replied_by(p).wait_recv())
    rows = rows_ref[...].reshape(SLOTS, RANK)
    residual = light_weight * (1.0 - rows_by_rows(factors[:LIGHT, :], rows))
    right_ref[...] = normals(flat_ref, rows_by_rows(pick, rows), light_weight, residual)
    keep = pltpu.make_async_copy(flat_ref, flat_out, load_sem.at[0])
    keep.start()

    for later, earlier in FORWARD:
        ahead(later, earlier).wait_send()
    for index, (at, e) in enumerate(leaves):
        owner, copy = leaf(index)
        if e != 0:
            copy.wait_send()
        else:
            pl.when(owner != r)(copy.wait_send)
    for sent in (ask, reply, give, burden, share_sum):
        peers(lambda p, sent=sent: sent(p).wait_send())

    peers(lambda p: sent_by(p).wait_recv())
    reduced_ref[...] = jnp.sum(landed[...], axis=0)
    peers(lambda p: sum_of(p).wait_recv())
    for k in range(n):
        a, b, c = k // 4, (k // 2) % 2, k % 2
        gram_ref[8 * a + 4 * c : 8 * a + 4 * c + 4, 128 * b : 128 * b + 128] = sum_in[k]
    peers(lambda p: send(p).wait_send())
    keep.wait()


def gather(n, items, requests, slots, confidence, block_user, counts, light, heavy, column_block):
    share = items.shape[0] // n
    blocks = slots.shape[0]
    users = LIGHT + HEAVY
    dma = [pltpu.SemaphoreType.DMA((n,)) for _ in range(14)]
    return pl.pallas_call(
        functools.partial(gather_kernel, n),
        out_shape=(
            jax.ShapeDtypeStruct((ENTRIES, 128), F32),
            jax.ShapeDtypeStruct((COLS, 128), F32),
            jax.ShapeDtypeStruct((MESSAGE, 128), F32),
            jax.ShapeDtypeStruct((COLS, RANK), F32),
        ),
        in_specs=[SMEM] + [HBM] * 8,
        out_specs=(HBM, VMEM, VMEM, VMEM),
        scratch_shapes=[
            pltpu.VMEM((ENTRIES, 128), F32),
            pltpu.VMEM((ENTRIES, 128), F32),
            pltpu.VMEM((n, CAP, 128), F32),
            pltpu.VMEM((n, CAP, 128), F32),
            pltpu.VMEM((1, 4, 128), F32),
            pltpu.VMEM((n, 4, 128), F32),
            pltpu.VMEM((len(SPINE), share, RANK), F32),
            pltpu.VMEM((n, share, RANK), F32),
            pltpu.VMEM((n, CAP, RANK), F32),
            pltpu.VMEM((n, CAP, RANK), F32),
            pltpu.VMEM((n, 1, 128), F32),
            pltpu.VMEM((n, 1, 128), F32),
            pltpu.VMEM((n, 4, 128), F32),
            pltpu.VMEM((n, 4, 128), F32),
            pltpu.VMEM((n, MESSAGE, 128), F32),
            pltpu.VMEM((n, MESSAGE, 128), F32),
            pltpu.VMEM((n * CAP, SLOTS), BF16),
            pltpu.VMEM((blocks, SLOTS), F32),
            pltpu.VMEM(requests.shape, jnp.int32),
            pltpu.VMEM(slots.shape, jnp.int32),
            pltpu.VMEM(slots.shape, F32),
            pltpu.VMEM((1, blocks), jnp.int32),
            pltpu.VMEM(counts.shape, jnp.int32),
            pltpu.VMEM((users, RANK), F32),
            pltpu.SemaphoreType.DMA((8,)),
            pltpu.SemaphoreType.DMA((len(SPINE),)),
            pltpu.SemaphoreType.DMA((len(SPINE),)),
            *dma,
        ],
        compiler_params=pltpu.CompilerParams(collective_id=0, has_side_effects=True, vmem_limit_bytes=LIMIT),
        name="gather",
    )(column_block, items, requests, slots, confidence, block_user, counts, light, heavy)


def solve_kernel(
    prior,
    cb_ref,
    flat_in,
    right_ref,
    heavy_sum_ref,
    gram_ref,
    light_ref,
    heavy_ref,
    light_out,
    heavy_out,
    flat_ref,
    flat_sem,
    a_ref,
    l_ref,
    inv_ref,
    x_ref,
):
    flat_load = pltpu.make_async_copy(flat_in, flat_ref, flat_sem)
    flat_load.start()
    r = lax.axis_index("rep")
    pick = picker(cb_ref[0])
    own = heavy_ref[pl.ds(r, 1), :]
    factors = jnp.concatenate([light_ref[...], own, jnp.zeros((128 - LIGHT - 1, RANK), F32)], 0)
    gram = prior * gram_ref[...]
    block = rows_by_rows(gram, pick) + (iota((COLS, COLS), 0) == iota((COLS, COLS), 1)).astype(F32)
    pulled = rows_by_rows(gram + pick, factors)
    turned = jnp.concatenate([heavy_sum_ref[...], jnp.zeros((128 - MESSAGE, 128), F32)], 0).T
    lane = iota((1, 128), 1)
    is_light, is_heavy = lane < LIGHT, lane == LIGHT
    right = jnp.where(is_light, right_ref[...], jnp.where(is_heavy, turned[:COLS, LINES : LINES + 1], 0.0)) - pulled
    flat_load.wait()
    for q in range(LINES):
        part = flat_ref[128 * q : 128 * q + 128, :]
        flat_ref[128 * q : 128 * q + 128, :] = jnp.where(
            is_light, part, jnp.where(is_heavy, turned[:, q : q + 1], 0.0)
        )
    for i in range(COLS):
        b = i // TILE
        at = START[b] + (i - TILE * b) * WIDTH[b]
        a_ref[i, TILE * b : COLS, :] = flat_ref[at : at + WIDTH[b], :] + block[TILE * b :, i : i + 1]
        a_ref[i, COLS : COLS + TILE, :] = jnp.broadcast_to(right[i : i + 1, :], (TILE, 128))

    tiles = PANELS + 1
    for b in range(PANELS):
        base = TILE * b
        acc = {
            (k, t): a_ref[base + k, TILE * t : TILE * t + TILE, :] for k in range(TILE) for t in range(b, tiles)
        }
        for k in range(TILE):
            own_tile = acc[k, b]
            inv = 1.0 / jnp.broadcast_to(own_tile[k : k + 1], (TILE, 128))
            inv_ref[base + k] = inv
            for t in range(b, tiles):
                if t > b:
                    a_ref[base + k, TILE * t : TILE * t + TILE, :] = acc[k, t]
                    if t < PANELS:
                        l_ref[base + k, TILE * t : TILE * t + TILE, :] = acc[k, t] * inv
            a_ref[base + k, base : base + TILE, :] = own_tile
            for k2 in range(k + 1, TILE):
                factor = jnp.broadcast_to(own_tile[k2 : k2 + 1], (TILE, 128)) * inv
                for t in range(b, tiles):
                    acc[k2, t] = acc[k2, t] - factor * acc[k, t]
        for s in range(b + 1, PANELS):
            for k2 in range(TILE):
                row = TILE * s + k2
                factors_ = [
                    jnp.broadcast_to(l_ref[base + k, row : row + 1, :], (TILE, 128)) for k in range(TILE)
                ]
                for t in range(s, tiles):
                    total = a_ref[row, TILE * t : TILE * t + TILE, :]
                    for k in range(TILE):
                        total = total - factors_[k] * a_ref[base + k, TILE * t : TILE * t + TILE, :]
                    a_ref[row, TILE * t : TILE * t + TILE, :] = total

    x = [None] * PANELS
    place = iota((TILE, 128), 0)
    for b in reversed(range(PANELS)):
        base = TILE * b
        left = []
        for k in range(TILE):
            value = a_ref[base + k, COLS : COLS + TILE, :]
            if b + 1 < PANELS:
                total = sum(
                    a_ref[base + k, TILE * t : TILE * t + TILE, :] * x[t] for t in range(b + 1, PANELS)
                )
                value = value - jnp.sum(total, axis=0, keepdims=True)
            left.append(value)
        found = jnp.zeros((TILE, 128), F32)
        for k in reversed(range(TILE)):
            value = left[k] * inv_ref[base + k]
            found = jnp.where(place == k, value, found)
            for k2 in range(k):
                left[k2] = left[k2] - jnp.broadcast_to(a_ref[base + k2, base + k : base + k + 1, :], (TILE, 128)) * value
        x[b] = found
        x_ref[base : base + TILE, :] = found
    x_ref[COLS:, :] = jnp.zeros((128 - COLS, 128), F32)
    delta = x_ref[...].T[:, :COLS]
    delta = jnp.concatenate([delta, delta, delta, delta], 1)
    inside = iota((1, RANK), 1) // COLS == cb_ref[0]
    light_out[...] = light_ref[...] + jnp.where(inside, delta[:LIGHT], 0.0)
    heavy_out[...] = own + jnp.where(inside, delta[LIGHT : LIGHT + 1], 0.0)


def solve(prior, flat, right, heavy_sum, gram, light, heavy, column_block):
    return pl.pallas_call(
        functools.partial(solve_kernel, prior),
        out_shape=(jax.ShapeDtypeStruct((LIGHT, RANK), F32), jax.ShapeDtypeStruct((1, RANK), F32)),
        in_specs=[SMEM, HBM, VMEM, VMEM, VMEM, VMEM, VMEM],
        out_specs=(VMEM, VMEM),
        scratch_shapes=[
            pltpu.VMEM((ENTRIES, 128), F32),
            pltpu.SemaphoreType.DMA(()),
            pltpu.VMEM((COLS, COLS + TILE, 128), F32),
            pltpu.VMEM((COLS, COLS, 128), F32),
            pltpu.VMEM((COLS, TILE, 128), F32),
            pltpu.VMEM((128, 128), F32),
        ],
        compiler_params=pltpu.CompilerParams(vmem_limit_bytes=LIMIT),
        name="solve",
    )(column_block, flat, right, heavy_sum, gram, light, heavy)


def local(items, light, heavy, requests, counts, slots, confidence, block_user, column_block):
    n = lax.axis_size("grp")
    blocks = block_user.shape[0]
    flat, right, heavy_sum, gram = gather(
        n,
        items,
        requests.T,
        slots.reshape(blocks, -1),
        confidence.reshape(blocks, -1),
        block_user.reshape(1, blocks),
        counts,
        light,
        heavy,
        column_block,
    )
    prior = UNOBSERVED / (items.shape[0] * n)
    return solve(prior, flat, right, heavy_sum, gram, light, heavy, column_block)


def solution(mesh):
    both = ("grp", "rep")
    return jax.shard_map(
        local,
        mesh=mesh,
        in_specs=(
            P("grp", None),
            P(both, None),
            P("grp", None),
            P(both, None),
            P(both, None),
            P(both),
            P(both),
            P(both),
            P(),
        ),
        out_specs=(P(both, None), P(both, None)),
        check_vma=False,
    )
```

```python
import functools

import jax
import jax.numpy as jnp
from jax import lax
from jax.experimental import pallas as pl
from jax.experimental.pallas import tpu as pltpu
from jax.sharding import PartitionSpec as P

COLS = 64
RANK = 256
SLOTS = 512
CAP = 16
LIGHT = 16
HEAVY = 32
TILE = 8
PANELS = COLS // TILE
UNOBSERVED = 128.0
MESH = pl.DeviceIdType.MESH
F32 = jnp.float32
BF16 = jnp.bfloat16
HIGHEST = lax.Precision.HIGHEST
VMEM = pl.BlockSpec(memory_space=pltpu.VMEM)
SMEM = pl.BlockSpec(memory_space=pltpu.SMEM)
HBM = pl.BlockSpec(memory_space=pltpu.HBM)
LIMIT = 56 * 1024 * 1024

WIDTH = [COLS - TILE * b for b in range(PANELS)]
START = [sum(TILE * w for w in WIDTH[:b]) for b in range(PANELS)]
ENTRIES = sum(TILE * w for w in WIDTH)
LINES = ENTRIES // 128
MESSAGE = 24

SPINE = [0, 7, 14, -7, -14]
FORWARD = [(1, 0), (3, 0), (2, 1), (4, 3)]
REACH = [0, 7, 14]
LEAVES = [(0, 1, -1, 2, -2, 3, -3)] * 2 + [(2, -3, 1, -2, 0, -1)] + [(0, 1, -1, 2, -2, 3, -3), (3, -1, 2, 0, 1)]


def iota(shape, dim):
    return lax.broadcasted_iota(jnp.int32, shape, dim)


def rows_by_rows(a, b, precision=HIGHEST):
    return lax.dot_general(a, b, (((1,), (1,)), ((), ())), precision=precision, preferred_element_type=F32)


def split(x, parts):
    out = []
    for _ in range(parts):
        part = x.astype(BF16)
        out.append(part)
        x = x - part.astype(F32)
    return out


def picker(column_block):
    return (iota((COLS, RANK), 1) == iota((COLS, RANK), 0) + column_block * COLS).astype(F32)


def gather_kernel(
    n,
    cb_ref,
    items_ref,
    req_ref,
    slots_ref,
    conf_ref,
    user_ref,
    counts_ref,
    light_ref,
    heavy_ref,
    flat_out,
    right_ref,
    reduced_ref,
    gram_ref,
    flat_ref,
    heavy_flat,
    load_out,
    load_in,
    sum_out,
    sum_in,
    spine,
    owned,
    answer,
    rows_ref,
    ask_out,
    ask_in,
    part_out,
    part_in,
    msg,
    landed,
    hot_ref,
    by_block,
    req_buf,
    slots_buf,
    conf_buf,
    user_buf,
    counts_buf,
    factors,
    load_sem,
    spine_s,
    spine_r,
    leaf_s,
    own_r,
    ask_s,
    ask_r,
    ans_s,
    ans_r,
    part_s,
    part_r,
    msg_s,
    msg_r,
    load_s,
    load_r,
    sum_s,
    sum_r,
):
    g, r = lax.axis_index("grp"), lax.axis_index("rep")
    share = owned.shape[1]
    users = LIGHT + HEAVY

    def plane(k):
        return lax.rem(g + (k + n), n)

    def put(src, dst, send, recv, target):
        return pltpu.make_async_remote_copy(
            src_ref=src, dst_ref=dst, send_sem=send, recv_sem=recv, device_id=target, device_id_type=MESH
        )

    def peers(body):
        def one(k, carry):
            body(lax.rem(r + k, n))
            return carry

        lax.fori_loop(1, n, one, 0)

    off = lax.rem(g + n - r, n)
    behind = off // (n // 2 + 1)
    size = off + behind * (n - 2 * off)
    level = (size + 3) // 7
    step = 7 * level
    source = lax.rem(r + step * (1 - 2 * behind) + n, n)

    barrier = pltpu.get_barrier_semaphore()

    @pl.when(source != g)
    def _():
        def greet(k, carry):
            pl.semaphore_signal(barrier, inc=1, device_id=(source, k), device_id_type=MESH)
            return carry

        lax.fori_loop(0, n, greet, 0)

    for hop in (7, -7):
        pl.semaphore_signal(barrier, inc=1, device_id=(plane(hop), r), device_id_type=MESH)
    peers(lambda p: pl.semaphore_signal(barrier, inc=1, device_id=(g, p), device_id_type=MESH))
    loads = [
        (items_ref.at[pl.ds(pl.multiple_of(r * share, share), share)], spine.at[0]),
        (req_ref, req_buf),
        (slots_ref, slots_buf),
        (conf_ref, conf_buf),
        (user_ref, user_buf),
        (counts_ref, counts_buf),
        (light_ref, factors.at[pl.ds(0, LIGHT)]),
        (heavy_ref, factors.at[pl.ds(LIGHT, HEAVY)]),
    ]
    loads = [pltpu.make_async_copy(src, dst, load_sem.at[k]) for k, (src, dst) in enumerate(loads)]
    for load in loads:
        load.start()

    leaves = [(k, e) for k in range(len(SPINE)) for e in LEAVES[k]]
    loads[1].wait()
    spread = (
        (iota((CAP, 128), 1) % CAP == iota((CAP, 128), 0)) & (iota((CAP, 128), 1) // CAP == lax.rem(r, TILE))
    ).astype(F32)
    asked = lax.dot_general(
        req_buf[...].astype(F32), spread, (((0,), (0,)), ((), ())), precision=HIGHEST, preferred_element_type=F32
    )
    for p in range(n):
        ask_out[p] = asked[p : p + 1, :]
    loads[0].wait()
    pl.semaphore_wait(barrier, n - 1 + 2 + sum(e != 0 for _, e in leaves))

    def ahead(k, from_k):
        hop = SPINE[k] - SPINE[from_k]
        return put(spine.at[from_k], spine.at[k], spine_s.at[k], spine_r.at[k], (plane(hop), r))

    def leaf(index):
        k, e = leaves[index]
        owner = plane(-SPINE[k])
        return owner, put(spine.at[k], owned.at[r], leaf_s.at[0], own_r.at[0], (plane(e), owner))

    def pass_on(k):
        for later, earlier in FORWARD:
            if earlier == k:
                ahead(later, k).start()
        for index, (at, e) in enumerate(leaves):
            if at != k:
                continue
            owner, copy = leaf(index)
            if e != 0:
                copy.start()
                continue

            @pl.when(owner != r)
            def _(copy=copy):
                copy.start()

            @pl.when(owner == r)
            def _():
                owned[r] = spine[k]

    def ask(p):
        return put(ask_out.at[p], ask_in.at[r], ask_s.at[0], ask_r.at[0], (g, p))

    def all_asks():
        return put(ask_out.at[pl.ds(0, n - 1)], ask_in.at[pl.ds(0, n - 1)], ask_s.at[0], ask_r.at[0], (g, lax.rem(r + 1, n)))

    pass_on(0)
    peers(lambda p: ask(p).start())
    ask_in[r] = ask_out[r]

    def weigh(step, carry):
        for k in range(4):
            row = 4 * step + k
            slot = slots_buf[pl.ds(row, 1), :]
            parts = [part.astype(F32) for part in split(conf_buf[pl.ds(row, 1), :], 3)]
            place = iota((16, 128), 0)
            parts = jnp.where(
                place < 4, parts[0], jnp.where(place < 8, parts[1], jnp.where(place < 12, parts[2], 0.0))
            )
            lhs = jnp.where((place & 3) == (slot >> 7), parts, 0.0).astype(BF16)
            hot = (iota((128, 128), 0) == (slot & 127)).astype(F32).astype(BF16)
            got = rows_by_rows(lhs, hot, None)
            got = got[0:4] + got[4:8] + got[8:12]
            by_block[pl.ds(row, 1), :] = jnp.concatenate([got[a : a + 1] for a in range(4)], 1)
        return carry

    for load in loads[2:]:
        load.wait()
    lax.fori_loop(0, by_block.shape[0] // 4, weigh, 0)

    all_asks().wait_recv()
    lines = [jnp.sum(ask_in[TILE * q : TILE * q + TILE], axis=0) for q in range(n // TILE)]
    lines = jnp.concatenate(lines + [jnp.zeros((TILE - len(lines), 128), F32)], 0)
    eye = (iota((128, 128), 0) == iota((128, 128), 1)).astype(F32)
    wanted = rows_by_rows(eye, lines)
    for q in range(n // TILE):
        hot_ref[128 * q : 128 * q + 128, :] = (
            (wanted[:, q : q + 1] == iota((128, SLOTS), 1).astype(F32)).astype(F32).astype(BF16)
        )

    def reply(p):
        return put(answer.at[p], rows_ref.at[r], ans_s.at[0], ans_r.at[0], (g, p))

    def all_replies():
        return put(answer.at[pl.ds(0, n - 1)], rows_ref.at[pl.ds(0, n - 1)], ans_s.at[0], ans_r.at[0], (g, lax.rem(r + 1, n)))

    pick = picker(cb_ref[0])

    def give(p):
        return put(part_out.at[p], part_in.at[r], part_s.at[0], part_r.at[0], (g, p))

    def all_parts():
        return put(part_out.at[pl.ds(0, n - 1)], part_in.at[pl.ds(0, n - 1)], part_s.at[0], part_r.at[0], (g, lax.rem(r + 1, n)))

    def stand_in():
        @pl.when(source == g)
        def _():
            put(owned.at[pl.ds(0, n - 1)], owned.at[pl.ds(0, n - 1)], leaf_s.at[0], own_r.at[0], (plane(1), r)).wait_recv()

        @pl.when(source != g)
        def _():
            put(owned, owned, leaf_s.at[0], own_r.at[0], (plane(1), r)).wait_recv()

        parts = split(owned[...].reshape(n * share, RANK), 2)
        half = n // 2

        def block(q, carry):
            at = lax.rem(r // half + 1 + q, 2)
            hot = hot_ref[pl.ds(pl.multiple_of(CAP * half * at, CAP * half), CAP * half), :]
            got = sum(jnp.dot(hot, part, preferred_element_type=F32) for part in parts)
            answer[pl.ds(pl.multiple_of(half * at, half), half)] = got.reshape(half, CAP, RANK)

            def one(k, inner):
                p = half * at + lax.rem(r + k, half)

                @pl.when(p != r)
                def _():
                    reply(p).start()

                @pl.when(p == r)
                def _():
                    rows_ref[r] = answer[r]

                return inner

            return lax.fori_loop(0, half, one, carry)

        lax.fori_loop(0, 2, block, 0)

    def burden(p):
        return put(load_out.at[p], load_in.at[r], load_s.at[0], load_r.at[0], (g, p))

    def all_burdens():
        return put(load_out.at[pl.ds(0, n - 1)], load_in.at[pl.ds(0, n - 1)], load_s.at[0], load_r.at[0], (g, lax.rem(r + 1, n)))

    for at in range(3):
        if at == 1:
            owners = counts_buf.shape[1]
            by_slot = (iota((owners, SLOTS), 1) // CAP == iota((owners, SLOTS), 0)).astype(F32).astype(BF16)
            limit = jnp.dot(
                jnp.broadcast_to(counts_buf[...], (TILE, owners)).astype(F32).astype(BF16),
                by_slot,
                preferred_element_type=F32,
            )[:1]
            live = (iota((1, SLOTS), 1) % CAP).astype(F32) < limit
            of_user = (iota((users, by_block.shape[0]), 0) == user_buf[...]).astype(F32)
            weight = jnp.dot(of_user, by_block[...], precision=HIGHEST, preferred_element_type=F32)
            weight = jnp.where(live, weight, 0.0)
            light_weight = weight[:LIGHT]
            turned = jnp.concatenate([weight[LIGHT:], jnp.zeros((128 - HEAVY, SLOTS), F32)], 0).T
            load_out[...] = turned.reshape(n, CAP, 128)
            peers(lambda p: burden(p).start())
            load_in[r] = load_out[r]
        if at < 2:
            for later, earlier in FORWARD:
                if abs(SPINE[later]) == REACH[at + 1]:
                    hop = SPINE[later] - SPINE[earlier]
                    put(
                        spine.at[earlier], spine.at[later], spine_s.at[later], spine_r.at[later], (plane(-hop), r)
                    ).wait_recv()
                    pass_on(later)
        if at == 2:
            all_burdens().wait_recv()
            heavy_weight = load_in[...].reshape(n * CAP, 128).T[:HEAVY]
            parts = jnp.concatenate([part.astype(F32) for part in split(heavy_weight, 3)], 0).astype(BF16)
            heavy_weight = jnp.dot(parts, hot_ref[...], preferred_element_type=F32)
            heavy_weight = (
                heavy_weight[:HEAVY] + heavy_weight[HEAVY : 2 * HEAVY] + heavy_weight[2 * HEAVY :]
            )
        pl.when(level == at)(stand_in)

    def all_sums():
        return put(sum_in.at[pl.ds(0, n - 1)], sum_in.at[pl.ds(0, n - 1)], sum_s.at[0], sum_r.at[0], (g, lax.rem(r + 1, n)))

    def share_sum(p):
        return put(sum_out.at[0], sum_in.at[r], sum_s.at[0], sum_r.at[0], (g, p))

    def send(p):
        return put(msg.at[p], landed.at[r], msg_s.at[0], msg_r.at[0], (g, p))

    def all_messages():
        return put(msg.at[pl.ds(0, n - 1)], landed.at[pl.ds(0, n - 1)], msg_s.at[0], msg_r.at[0], (g, lax.rem(r + 1, n)))

    def normals(into, cols, weight, residual):
        count = weight.shape[0]
        none = jnp.zeros((64 - count, SLOTS), F32)
        high, low = [part.astype(F32) for part in split(weight, 2)]
        both = jnp.concatenate([high, none, low, none], 0).astype(BF16)
        once = jnp.concatenate([high, none, jnp.zeros((64, SLOTS), F32)], 0).astype(BF16)
        for b in range(PANELS):
            width = WIDTH[b]
            tail = cols[TILE * b :]
            product = jnp.concatenate([tail * cols[TILE * b + i : TILE * b + i + 1] for i in range(TILE)], 0)
            p_high, p_low = split(product, 2)
            first = rows_by_rows(p_high, both, None)
            second = rows_by_rows(p_low, once, None)
            into[START[b] : START[b] + TILE * width, :] = first + pltpu.roll(first, 64, 1) + second
        return rows_by_rows(cols, jnp.concatenate([residual, jnp.zeros((128 - count, SLOTS), F32)], 0))

    mine = owned[...].reshape(n * share, RANK)
    cols = rows_by_rows(pick, mine)
    part = jnp.dot(cols, mine, precision=HIGHEST, preferred_element_type=F32)
    for k in range(n):
        a, b, c = k // 4, (k // 2) % 2, k % 2
        part_out[k] = part[8 * a + 4 * c : 8 * a + 4 * c + 4, 128 * b : 128 * b + 128]
    peers(lambda p: give(p).start())
    part_in[r] = part_out[r]

    residual = heavy_weight * (1.0 - rows_by_rows(factors[LIGHT:users, :], mine))
    right = normals(heavy_flat, cols, heavy_weight, residual)
    for q in range(LINES):
        msg[:, q, :] = heavy_flat[128 * q : 128 * q + 128, :].T[:HEAVY]
    msg[:, LINES, :] = jnp.concatenate([right, jnp.zeros((64, 128), F32)], 0).T[:HEAVY]
    for q in range(LINES + 1, MESSAGE):
        msg[:, q, :] = jnp.zeros((HEAVY, 128), F32)
    peers(lambda p: send(p).start())
    landed[r] = msg[r]

    all_parts().wait_recv()
    sum_out[0] = jnp.sum(part_in[...], axis=0)
    peers(lambda p: share_sum(p).start())
    sum_in[r] = sum_out[0]

    all_replies().wait_recv()
    rows = rows_ref[...].reshape(SLOTS, RANK)
    residual = light_weight * (1.0 - rows_by_rows(factors[:LIGHT, :], rows))
    right_ref[...] = normals(flat_ref, rows_by_rows(pick, rows), light_weight, residual)
    keep = pltpu.make_async_copy(flat_ref, flat_out, load_sem.at[0])
    keep.start()

    for later, earlier in FORWARD:
        ahead(later, earlier).wait_send()
    @pl.when(source == g)
    def _():
        put(owned.at[pl.ds(0, n - 1)], owned.at[pl.ds(0, n - 1)], leaf_s.at[0], own_r.at[0], (plane(1), r)).wait_send()

    @pl.when(source != g)
    def _():
        put(owned, owned, leaf_s.at[0], own_r.at[0], (plane(1), r)).wait_send()

    for sent in (all_asks, all_replies, all_parts, all_burdens, all_sums):
        sent().wait_send()

    all_messages().wait_recv()
    reduced_ref[...] = jnp.sum(landed[...], axis=0)
    all_sums().wait_recv()
    for k in range(n):
        a, b, c = k // 4, (k // 2) % 2, k % 2
        gram_ref[8 * a + 4 * c : 8 * a + 4 * c + 4, 128 * b : 128 * b + 128] = sum_in[k]
    all_messages().wait_send()
    keep.wait()


def gather(n, items, requests, slots, confidence, block_user, counts, light, heavy, column_block):
    share = items.shape[0] // n
    blocks = slots.shape[0]
    users = LIGHT + HEAVY
    dma = [pltpu.SemaphoreType.DMA((n,)) for _ in range(14)]
    return pl.pallas_call(
        functools.partial(gather_kernel, n),
        out_shape=(
            jax.ShapeDtypeStruct((ENTRIES, 128), F32),
            jax.ShapeDtypeStruct((COLS, 128), F32),
            jax.ShapeDtypeStruct((MESSAGE, 128), F32),
            jax.ShapeDtypeStruct((COLS, RANK), F32),
        ),
        in_specs=[SMEM] + [HBM] * 8,
        out_specs=(HBM, VMEM, VMEM, VMEM),
        scratch_shapes=[
            pltpu.VMEM((ENTRIES, 128), F32),
            pltpu.VMEM((ENTRIES, 128), F32),
            pltpu.VMEM((n, CAP, 128), F32),
            pltpu.VMEM((n, CAP, 128), F32),
            pltpu.VMEM((1, 4, 128), F32),
            pltpu.VMEM((n, 4, 128), F32),
            pltpu.VMEM((len(SPINE), share, RANK), F32),
            pltpu.VMEM((n, share, RANK), F32),
            pltpu.VMEM((n, CAP, RANK), F32),
            pltpu.VMEM((n, CAP, RANK), F32),
            pltpu.VMEM((n, 1, 128), F32),
            pltpu.VMEM((n, 1, 128), F32),
            pltpu.VMEM((n, 4, 128), F32),
            pltpu.VMEM((n, 4, 128), F32),
            pltpu.VMEM((n, MESSAGE, 128), F32),
            pltpu.VMEM((n, MESSAGE, 128), F32),
            pltpu.VMEM((n * CAP, SLOTS), BF16),
            pltpu.VMEM((blocks, SLOTS), F32),
            pltpu.VMEM(requests.shape, jnp.int32),
            pltpu.VMEM(slots.shape, jnp.int32),
            pltpu.VMEM(slots.shape, F32),
            pltpu.VMEM((1, blocks), jnp.int32),
            pltpu.VMEM(counts.shape, jnp.int32),
            pltpu.VMEM((users, RANK), F32),
            pltpu.SemaphoreType.DMA((8,)),
            pltpu.SemaphoreType.DMA((len(SPINE),)),
            pltpu.SemaphoreType.DMA((len(SPINE),)),
            *dma,
        ],
        compiler_params=pltpu.CompilerParams(collective_id=0, has_side_effects=True, vmem_limit_bytes=LIMIT),
        name="gather",
    )(column_block, items, requests, slots, confidence, block_user, counts, light, heavy)


def solve_kernel(
    prior,
    cb_ref,
    flat_in,
    right_ref,
    heavy_sum_ref,
    gram_ref,
    light_ref,
    heavy_ref,
    light_out,
    heavy_out,
    flat_ref,
    flat_sem,
    a_ref,
    l_ref,
    inv_ref,
    x_ref,
):
    flat_load = pltpu.make_async_copy(flat_in, flat_ref, flat_sem)
    flat_load.start()
    r = lax.axis_index("rep")
    pick = picker(cb_ref[0])
    own = heavy_ref[pl.ds(r, 1), :]
    factors = jnp.concatenate([light_ref[...], own, jnp.zeros((128 - LIGHT - 1, RANK), F32)], 0)
    gram = prior * gram_ref[...]
    block = rows_by_rows(gram, pick) + (iota((COLS, COLS), 0) == iota((COLS, COLS), 1)).astype(F32)
    pulled = rows_by_rows(gram + pick, factors)
    turned = jnp.concatenate([heavy_sum_ref[...], jnp.zeros((128 - MESSAGE, 128), F32)], 0).T
    lane = iota((1, 128), 1)
    is_light, is_heavy = lane < LIGHT, lane == LIGHT
    right = jnp.where(is_light, right_ref[...], jnp.where(is_heavy, turned[:COLS, LINES : LINES + 1], 0.0)) - pulled
    flat_load.wait()
    for q in range(LINES):
        part = flat_ref[128 * q : 128 * q + 128, :]
        flat_ref[128 * q : 128 * q + 128, :] = jnp.where(
            is_light, part, jnp.where(is_heavy, turned[:, q : q + 1], 0.0)
        )
    for i in range(COLS):
        b = i // TILE
        at = START[b] + (i - TILE * b) * WIDTH[b]
        a_ref[i, TILE * b : COLS, :] = flat_ref[at : at + WIDTH[b], :] + block[TILE * b :, i : i + 1]
        a_ref[i, COLS : COLS + TILE, :] = jnp.broadcast_to(right[i : i + 1, :], (TILE, 128))

    tiles = PANELS + 1
    for b in range(PANELS):
        base = TILE * b
        acc = {
            (k, t): a_ref[base + k, TILE * t : TILE * t + TILE, :] for k in range(TILE) for t in range(b, tiles)
        }
        for k in range(TILE):
            own_tile = acc[k, b]
            inv = 1.0 / jnp.broadcast_to(own_tile[k : k + 1], (TILE, 128))
            inv_ref[base + k] = inv
            for t in range(b, tiles):
                if t > b:
                    a_ref[base + k, TILE * t : TILE * t + TILE, :] = acc[k, t]
                    if t < PANELS:
                        l_ref[base + k, TILE * t : TILE * t + TILE, :] = acc[k, t] * inv
            a_ref[base + k, base : base + TILE, :] = own_tile
            for k2 in range(k + 1, TILE):
                factor = jnp.broadcast_to(own_tile[k2 : k2 + 1], (TILE, 128)) * inv
                for t in range(b, tiles):
                    acc[k2, t] = acc[k2, t] - factor * acc[k, t]
        for s in range(b + 1, PANELS):
            for k2 in range(TILE):
                row = TILE * s + k2
                factors_ = [
                    jnp.broadcast_to(l_ref[base + k, row : row + 1, :], (TILE, 128)) for k in range(TILE)
                ]
                for t in range(s, tiles):
                    total = a_ref[row, TILE * t : TILE * t + TILE, :]
                    for k in range(TILE):
                        total = total - factors_[k] * a_ref[base + k, TILE * t : TILE * t + TILE, :]
                    a_ref[row, TILE * t : TILE * t + TILE, :] = total

    x = [None] * PANELS
    place = iota((TILE, 128), 0)
    for b in reversed(range(PANELS)):
        base = TILE * b
        left = []
        for k in range(TILE):
            value = a_ref[base + k, COLS : COLS + TILE, :]
            if b + 1 < PANELS:
                total = sum(
                    a_ref[base + k, TILE * t : TILE * t + TILE, :] * x[t] for t in range(b + 1, PANELS)
                )
                value = value - jnp.sum(total, axis=0, keepdims=True)
            left.append(value)
        found = jnp.zeros((TILE, 128), F32)
        for k in reversed(range(TILE)):
            value = left[k] * inv_ref[base + k]
            found = jnp.where(place == k, value, found)
            for k2 in range(k):
                left[k2] = left[k2] - jnp.broadcast_to(a_ref[base + k2, base + k : base + k + 1, :], (TILE, 128)) * value
        x[b] = found
        x_ref[base : base + TILE, :] = found
    x_ref[COLS:, :] = jnp.zeros((128 - COLS, 128), F32)
    delta = x_ref[...].T[:, :COLS]
    delta = jnp.concatenate([delta, delta, delta, delta], 1)
    inside = iota((1, RANK), 1) // COLS == cb_ref[0]
    light_out[...] = light_ref[...] + jnp.where(inside, delta[:LIGHT], 0.0)
    heavy_out[...] = own + jnp.where(inside, delta[LIGHT : LIGHT + 1], 0.0)


def solve(prior, flat, right, heavy_sum, gram, light, heavy, column_block):
    return pl.pallas_call(
        functools.partial(solve_kernel, prior),
        out_shape=(jax.ShapeDtypeStruct((LIGHT, RANK), F32), jax.ShapeDtypeStruct((1, RANK), F32)),
        in_specs=[SMEM, HBM, VMEM, VMEM, VMEM, VMEM, VMEM],
        out_specs=(VMEM, VMEM),
        scratch_shapes=[
            pltpu.VMEM((ENTRIES, 128), F32),
            pltpu.SemaphoreType.DMA(()),
            pltpu.VMEM((COLS, COLS + TILE, 128), F32),
            pltpu.VMEM((COLS, COLS, 128), F32),
            pltpu.VMEM((COLS, TILE, 128), F32),
            pltpu.VMEM((128, 128), F32),
        ],
        compiler_params=pltpu.CompilerParams(vmem_limit_bytes=LIMIT),
        name="solve",
    )(column_block, flat, right, heavy_sum, gram, light, heavy)


def local(items, light, heavy, requests, counts, slots, confidence, block_user, column_block):
    n = lax.axis_size("grp")
    blocks = block_user.shape[0]
    flat, right, heavy_sum, gram = gather(
        n,
        items,
        requests.T,
        slots.reshape(blocks, -1),
        confidence.reshape(blocks, -1),
        block_user.reshape(1, blocks),
        counts,
        light,
        heavy,
        column_block,
    )
    prior = UNOBSERVED / (items.shape[0] * n)
    return solve(prior, flat, right, heavy_sum, gram, light, heavy, column_block)


def solution(mesh):
    both = ("grp", "rep")
    return jax.shard_map(
        local,
        mesh=mesh,
        in_specs=(
            P("grp", None),
            P(both, None),
            P("grp", None),
            P(both, None),
            P(both, None),
            P(both),
            P(both),
            P(both),
            P(),
        ),
        out_specs=(P(both, None), P(both, None)),
        check_vma=False,
    )
```
